32 devices in a mesh: enc: 4 (over y, x), span: 8 (over z, core).
Axes of the slice: x: 2, y: 2, z: 4, core: 2. Of those that a mesh axis runs over, the one named last changes fastest.
Arguments:
- queries: bfloat16 [8192, 3072], P('span', 'enc'), may hold values from -6 to 6
- cotangent: bfloat16 [8192, 3072], P('span', 'enc'), may hold values from -12 to 12
- key_weight: bfloat16 [896, 3072], P(None, 'enc'), may hold values from -0.1875 to 0.1875
- value_weight: bfloat16 [896, 3072], P(None, 'enc'), may hold values from -0.75 to 0.75
- neighbour_store: bfloat16 [256, 128, 896], P('span', None, 'enc'), may hold values from -6 to 6
- block_scale: bfloat16 [256, 128], P('span'), may hold values from 0.5 to 2
- fetch_index: int32 [8, 8, 8], P('span'), may hold values from 0 to 31
- neighbour_slot: int32 [8, 32], P('span'), may hold values from 0 to 63, as said below
- second_valid: int32 [8, 16], P('span'), may hold values 0 or 1
- live_spans: int32 [8], P('span'), may hold values from 1 to 16, as said below
Outputs:
- attended: bfloat16 [8192, 3072], P('span', 'enc')
- grad_store: float32 [256, 128, 896], P('span', None, 'enc')
The draws below stay inside these ranges and needn't reach their ends.
Inputs may be any that keep to these rules, and one draw needn't show every extreme that they name: `fetch_index`: the local block, of the 32 of store shard c2, that it sends to owner shard c in slot s; slots that no neighbour names are padding. `neighbour_slot`: entry j * 2 + k of row c names the fetched slot c2 * 8 + s holding neighbour k of owner shard c's span j; no slot is named twice in a row; the slots named from store shard c2 are c2 * 8 to c2 * 8 + n - 1 for some count n of 0 to 8; in each row one store shard gives all 8 slots, and each store shard gives all 8 slots to some owner shard. Spans 0 to live_spans[c] - 1 of owner shard c are live, the others are padding; some shard has all 16 live.
All inputs are finite; a program needn't handle non-finite values. No bound on the sum of `second_valid` on one device may be relied on, other than what follows from the above.
Results may differ from the reference program's by a relative error of at most 0.012.
The reference program's roundings to bfloat16 on the way count: a program that leaves them out, or rounds other values in their place, can miss the bound.
Values may be sent and summed in bfloat16 or wider, within the bound.
A program may use at most 192 MiB of HBM per device.

```python
import math
import jax
import jax.numpy as jnp
from jax import lax

HEADS = 24
HD = 128
ENC_D = 896
CL = 64
NT = 128
NBR = 2
CH = 16
BLK_DEV = 32
GROUPS = 4
SHARDS = 8
CAP = 8
TOKENS = 8192
BLOCKS = 256


def draw_live_spans(key, part):
    key = jax.random.fold_in(key, 7)
    first_key, second_key, third_key = jax.random.split(key, 3)
    first_draw = jax.random.randint(first_key, (SHARDS,), 0, CH)
    second_draw = jax.random.randint(second_key, (SHARDS,), 0, CH)
    busiest = jax.random.randint(third_key, (), 0, SHARDS)
    live_count = 1 + first_draw * second_draw // CH
    return jnp.where(jnp.arange(SHARDS) == busiest, CH, live_count).astype(jnp.int32)


def draw_neighbour_slot(key, part):
    key = jax.random.fold_in(key, 11)
    hot_key, weight_key, tie_key, order_key = jax.random.split(key, 4)
    hot_store = jax.random.permutation(hot_key, SHARDS).astype(jnp.int32)
    weight = jax.random.randint(weight_key, (SHARDS, SHARDS), 0, CAP).astype(jnp.int32)
    stores = jnp.arange(SHARDS, dtype=jnp.int32)
    weight = jnp.where(stores[None, :] == hot_store[:, None], 2 * CAP, weight).astype(jnp.int32)
    tie_keys = jax.random.split(tie_key, SHARDS)
    tie = jax.vmap(lambda one_key: jax.random.permutation(one_key, SHARDS))(tie_keys).astype(jnp.int32)
    slot_pos = jnp.arange(CAP, dtype=jnp.int32)
    score = (slot_pos[None, None, :] - weight[:, :, None]) * SHARDS + tie[:, :, None]
    flat_score = score.reshape(SHARDS, SHARDS * CAP)
    chosen = jnp.argsort(flat_score, axis=1)[:, :CH * NBR].astype(jnp.int32)
    order_keys = jax.random.split(order_key, SHARDS)
    order = jax.vmap(lambda one_key: jax.random.permutation(one_key, CH * NBR))(order_keys).astype(jnp.int32)
    return jnp.take_along_axis(chosen, order, axis=1).astype(jnp.int32)


def place_ends(values, own_key, smallest, top_value):
    spot = [jax.random.randint(jax.random.fold_in(own_key, axis), (), 0, length) for axis, length in enumerate(values.shape)]
    widest = values.shape.index(max(values.shape))
    beside = spot[:widest] + [(spot[widest] + 1) % values.shape[widest]] + spot[widest + 1:]
    return values.at[tuple(spot)].set(smallest).at[tuple(beside)].set(top_value)


def levels(own_key, dims, cuts, smallest, high):
    def one(position, shards_of):
        draws = jax.random.uniform(jax.random.fold_in(jax.random.fold_in(own_key, 6), position), (shards_of,), jnp.float32, smallest / len(cuts), high / len(cuts))
        return jnp.repeat(jnp.exp(draws), dims[position] // shards_of).reshape((-1,) + (1,) * (len(dims) - position - 1))

    gain = one(*cuts[0])
    for cut in cuts[1:]:
        gain = gain * one(*cut)
    return gain


def gaussian(own_key, shape, deviation, most, pieces=(), held_as=jnp.bfloat16):
    result = jax.random.normal(own_key, shape, jnp.float32) * deviation
    if len(pieces) > 0:
        result = levels(own_key, shape, pieces, -0.22, 0.18) * result
    return jnp.clip(result, min=-most, max=most).astype(held_as)


def setup_inputs(seed: int = 0) -> dict:
    key_list = jax.random.split(jax.random.key(seed), 11)
    queries = gaussian(key_list[0], (TOKENS, HEADS * HD), 1.0, 6.0, ((0, 8), (1, 4)))
    cotangent = gaussian(key_list[1], (TOKENS, HEADS * HD), 2.0, 12.0, ((0, 8), (1, 4)))
    key_weight = gaussian(key_list[2], (ENC_D, HEADS * HD), ENC_D ** -0.5, 0.1875, ((1, 4),))
    value_weight = gaussian(key_list[3], (ENC_D, HEADS * HD), (ENC_D // 16) ** -0.5, 0.75, ((1, 4),))
    neighbour_store = gaussian(key_list[4], (BLOCKS, NT, ENC_D), 1.0, 6.0, ((0, 8), (2, 4)))
    block_scale = jnp.clip(jnp.exp(math.log(2.0) - 1.3862944 * jax.random.uniform(key_list[5], (BLOCKS, NT), jnp.float32) ** levels(key_list[5], (BLOCKS, NT), ((0, 8),), -0.2, 0.2)), 0.5, 2.0).astype(jnp.bfloat16)
    fetch_index = place_ends(jax.random.randint(key_list[6], (SHARDS, SHARDS, CAP), 0, BLK_DEV), jax.random.fold_in(key_list[6], 1), 0, BLK_DEV - 1).astype(jnp.int32)
    neighbour_slot = draw_neighbour_slot(jax.random.fold_in(key_list[10], 71), 0)
    second_valid = place_ends((jax.random.randint(key_list[8], (SHARDS, CH), 0, 4) < 3).astype(jnp.int32), jax.random.fold_in(key_list[8], 1), 0, 1)
    live_spans = draw_live_spans(jax.random.fold_in(key_list[10], 71), 0)
    return {"queries": queries, "cotangent": cotangent, "key_weight": key_weight, "value_weight": value_weight, "neighbour_store": neighbour_store, "block_scale": block_scale, "fetch_index": fetch_index, "neighbour_slot": neighbour_slot, "second_valid": second_valid, "live_spans": live_spans}


def span_attention(query_part, cotangent_part, fetched, key_weight, value_weight, valid_row, live_count):
    flat_rows = fetched.reshape(CH * NBR * NT, ENC_D)
    key_proj = jnp.dot(flat_rows, key_weight, preferred_element_type=jnp.float32).astype(jnp.bfloat16)
    value_proj = jnp.dot(flat_rows, value_weight, preferred_element_type=jnp.float32).astype(jnp.bfloat16)
    keys_view = key_proj.reshape(CH, NBR * NT, HEADS, HD).astype(jnp.float32)
    values_view = value_proj.reshape(CH, NBR * NT, HEADS, HD).astype(jnp.float32)
    query_view = query_part.reshape(CH, CL, HEADS, HD).astype(jnp.float32)
    scale_factor = 1.0 / math.sqrt(HD)
    neighbour = jnp.arange(NBR * NT, dtype=jnp.int32) // NT
    key_mask = jnp.where(neighbour[None, :] == 0, 1.0, valid_row[:, None].astype(jnp.float32)).astype(jnp.float32)
    live_mask = jnp.arange(CH, dtype=jnp.int32) < live_count
    scores = jnp.einsum('cqhd,ckhd->chqk', query_view, keys_view) * scale_factor
    weights = jnp.exp(scores) * key_mask[:, None, None, :]
    probabilities = weights / lax.optimization_barrier(jnp.sum(weights, axis=-1, keepdims=True))
    probs_low = probabilities.astype(jnp.bfloat16)
    probs_wide = probs_low.astype(jnp.float32)
    mixture = jnp.einsum('chqk,ckhd->cqhd', probs_wide, values_view)
    attended = jnp.where(live_mask[:, None, None, None], mixture, 0.0).astype(jnp.bfloat16)
    grad_out = jnp.where(live_mask[:, None, None, None], cotangent_part.reshape(CH, CL, HEADS, HD), 0.0).astype(jnp.bfloat16)
    grad_wide = grad_out.astype(jnp.float32)
    grad_values = jnp.einsum('chqk,cqhd->ckhd', probs_wide, grad_wide).astype(jnp.bfloat16)
    grad_probs = jnp.einsum('cqhd,ckhd->chqk', grad_wide, values_view)
    inner_sum = lax.optimization_barrier(jnp.sum(probabilities * grad_probs, axis=-1, keepdims=True))
    grad_scores = (probabilities * (grad_probs - inner_sum) * scale_factor).astype(jnp.bfloat16)
    grad_keys = jnp.einsum('chqk,cqhd->ckhd', grad_scores.astype(jnp.float32), query_view).astype(jnp.bfloat16)
    group_width = HEADS * HD // GROUPS
    key_groups = grad_keys.reshape(CH * NBR * NT, GROUPS, group_width).astype(jnp.float32)
    value_groups = grad_values.reshape(CH * NBR * NT, GROUPS, group_width).astype(jnp.float32)
    key_split = key_weight.reshape(ENC_D, GROUPS, group_width).astype(jnp.float32)
    value_split = value_weight.reshape(ENC_D, GROUPS, group_width).astype(jnp.float32)
    partial_value = jnp.einsum('rgw,fgw->grf', key_groups, key_split) + jnp.einsum('rgw,fgw->grf', value_groups, value_split)
    partial_value = partial_value.astype(jnp.bfloat16)
    slot_grad = lax.optimization_barrier(jnp.sum(partial_value.astype(jnp.float32), axis=0))
    return (attended.reshape(CH * CL, HEADS * HD), slot_grad.reshape(CH * NBR, NT, ENC_D))

def reference(queries, cotangent, key_weight, value_weight, neighbour_store, block_scale, fetch_index, neighbour_slot, second_valid, live_spans):
    encoded = (neighbour_store.astype(jnp.float32) * block_scale.astype(jnp.float32)[:, :, None]).astype(jnp.bfloat16)
    block_base = (jnp.arange(SHARDS, dtype=jnp.int32) * BLK_DEV)[None, :, None]
    slot_block = (jnp.transpose(fetch_index, (1, 0, 2)) + block_base).reshape(SHARDS, SHARDS * CAP).astype(jnp.int32)
    block_of = jnp.take_along_axis(slot_block, neighbour_slot, axis=1).astype(jnp.int32)
    query_parts = queries.reshape(SHARDS, CH * CL, HEADS * HD)
    cotangent_parts = cotangent.reshape(SHARDS, CH * CL, HEADS * HD)

    def advance(running, inputs):
        query_part, cotangent_part, blocks, valid_row, live_count = inputs
        fetched = jnp.take(encoded, blocks, axis=0)
        attended, slot_grad = span_attention(query_part, cotangent_part, fetched, key_weight, value_weight, valid_row, live_count)
        running = running.at[blocks].add(slot_grad)
        return (running, attended)
    start_total = jnp.zeros((BLOCKS, NT, ENC_D), jnp.float32)
    running, attended = lax.scan(advance, start_total, (query_parts, cotangent_parts, block_of, second_valid, live_spans))
    grad_store = running * block_scale.astype(jnp.float32)[:, :, None]
    return (attended.reshape(TOKENS, HEADS * HD), grad_store)
```

```python
import functools
import math

import jax
import jax.numpy as jnp
from jax import lax
from jax.experimental import pallas as pl
from jax.experimental.pallas import tpu as pltpu
from jax.sharding import PartitionSpec as P

HD = 128
CL = 64
NT = 128
NBR = 2
SPANS_PER_STEP = 2
VMEM_BYTES = 56 * 1024 * 1024

VMEM = pl.BlockSpec(memory_space=pltpu.VMEM)
SMEM = pl.BlockSpec(memory_space=pltpu.SMEM)


def params(**kw):
    return pltpu.CompilerParams(vmem_limit_bytes=VMEM_BYTES, **kw)


def pack_kernel(served_ref, store_ref, scale_ref, out_ref, encoded):
    blocks = store_ref.shape[0]

    def encode(b, carry):
        wide = store_ref[b].astype(jnp.float32)
        scaled = wide.T * scale_ref[pl.ds(b, 1), :]
        encoded[b] = scaled.astype(jnp.bfloat16)
        return carry

    lax.fori_loop(0, blocks, encode, 0)

    def copy(p, carry):
        out_ref[p] = encoded[served_ref[p]]
        return carry

    lax.fori_loop(0, out_ref.shape[0], copy, 0)


def pick_kernel(order_ref, in_ref, out_ref):
    def copy(i, carry):
        out_ref[i] = in_ref[order_ref[i]]
        return carry

    lax.fori_loop(0, out_ref.shape[0], copy, 0)


def attend_kernel(
    valid_ref,
    live_ref,
    x_ref,
    q_ref,
    c_ref,
    wkt_ref,
    wvt_ref,
    wk_ref,
    wv_ref,
    att_ref,
    part_ref,
    grad_k,
    grad_v,
):
    step = pl.program_id(0)
    heads = q_ref.shape[1] // HD
    enc, _, features, _ = x_ref.shape
    scale_factor = 1.0 / math.sqrt(HD)
    cols = lax.broadcasted_iota(jnp.int32, (1, NBR * NT), 1)
    dims_t = (((0,), (0,)), ((), ()))
    dims_nt = (((1,), (1,)), ((), ()))
    f32 = jnp.float32
    for j in range(SPANS_PER_STEP):
        span = step * SPANS_PER_STEP + j
        second = valid_ref[span].astype(f32)
        live = span < live_ref[0]
        mask = jnp.where(cols < NT, 1.0, second)
        halves = [x_ref[:, NBR * j + k].reshape(enc * features, NT) for k in range(NBR)]
        x = jnp.concatenate(halves, axis=1)
        key_t = jnp.dot(wkt_ref[...], x, preferred_element_type=f32).astype(jnp.bfloat16)
        value_t = jnp.dot(wvt_ref[...], x, preferred_element_type=f32).astype(jnp.bfloat16)
        rows = slice(j * CL, (j + 1) * CL)
        for h in range(heads):
            head = slice(h * HD, (h + 1) * HD)
            q = q_ref[rows, head]
            go = c_ref[rows, head]
            go = jnp.where(live, go, jnp.zeros_like(go))
            k_t = key_t[head, :]
            v_t = value_t[head, :]
            scores = jnp.dot(q, k_t, preferred_element_type=f32) * scale_factor
            weights = jnp.exp(scores) * mask
            probs = weights / jnp.sum(weights, axis=1, keepdims=True)
            low = probs.astype(jnp.bfloat16)
            mixture = lax.dot_general(low, v_t, dims_nt, preferred_element_type=f32)
            att_ref[rows, head] = jnp.where(live, mixture, 0.0).astype(jnp.bfloat16)
            grad_v[j, head, :] = lax.dot_general(
                go, low, dims_t, preferred_element_type=f32
            ).astype(jnp.bfloat16)
            grad_p = jnp.dot(go, v_t, preferred_element_type=f32)
            inner = jnp.sum(probs * grad_p, axis=1, keepdims=True)
            grad_s = (probs * (grad_p - inner) * scale_factor).astype(jnp.bfloat16)
            grad_k[j, head, :] = lax.dot_general(
                q, grad_s, dims_t, preferred_element_type=f32
            ).astype(jnp.bfloat16)
        part = jnp.dot(wk_ref[...], grad_k[j], preferred_element_type=f32)
        part = part + jnp.dot(wv_ref[...], grad_v[j], preferred_element_type=f32)
        part = part.astype(jnp.bfloat16)
        for k in range(NBR):
            half = part[:, k * NT : (k + 1) * NT]
            part_ref[:, NBR * j + k] = half.reshape(enc, features, NT)


def merge_kernel(order_ref, in_ref, out_ref):
    out_ref[...] = jnp.zeros_like(out_ref)

    def put(i, carry):
        total = in_ref[0, i].astype(jnp.float32)
        for e in range(1, in_ref.shape[0]):
            total = total + in_ref[e, i].astype(jnp.float32)
        out_ref[order_ref[i]] = total.astype(jnp.bfloat16)
        return carry

    lax.fori_loop(0, in_ref.shape[1], put, 0)


def gather_kernel(served_ref, in_ref, scale_ref, out_ref, total):
    total[...] = jnp.zeros_like(total)

    def add(p, carry):
        b = served_ref[p]
        total[b] = total[b] + in_ref[p].astype(jnp.float32)
        return carry

    lax.fori_loop(0, in_ref.shape[0], add, 0)

    def write(b, carry):
        scaled = total[b] * scale_ref[pl.ds(b, 1), :]
        out_ref[b] = scaled.T
        return carry

    lax.fori_loop(0, out_ref.shape[0], write, 0)


def per_device(
    queries,
    cotangent,
    key_weight,
    value_weight,
    neighbour_store,
    block_scale,
    fetch_index,
    neighbour_slot,
    second_valid,
    live_spans,
):
    enc_count = lax.axis_size("enc")
    shard_count = lax.axis_size("span")
    slot_total = shard_count * fetch_index.shape[2]
    blocks_here, _, features = neighbour_store.shape
    enc_features, head_width = key_weight.shape
    slot_order = neighbour_slot[0]
    used_count = slot_order.shape[0]
    spans = used_count // NBR
    served = fetch_index[0].reshape(slot_total)
    scale_wide = block_scale.astype(jnp.float32)
    bf16 = jnp.bfloat16

    outgoing = pl.pallas_call(
        pack_kernel,
        out_shape=jax.ShapeDtypeStruct((slot_total, features, NT), bf16),
        in_specs=[SMEM, VMEM, VMEM],
        out_specs=VMEM,
        scratch_shapes=[pltpu.VMEM((blocks_here, features, NT), bf16)],
        compiler_params=params(),
    )(served, neighbour_store, scale_wide)
    received = lax.all_to_all(outgoing, "span", split_axis=0, concat_axis=0, tiled=True)
    arranged = pl.pallas_call(
        pick_kernel,
        out_shape=jax.ShapeDtypeStruct((used_count, features, NT), bf16),
        in_specs=[SMEM, VMEM],
        out_specs=VMEM,
        compiler_params=params(),
    )(slot_order, received)
    whole = lax.all_gather(arranged, "enc", axis=0, tiled=False)

    step_blocks = SPANS_PER_STEP * NBR
    step_rows = SPANS_PER_STEP * CL
    resident = lambda i, *_: (0, 0)
    by_rows = pl.BlockSpec((step_rows, head_width), lambda i, *_: (i, 0))
    by_blocks = pl.BlockSpec((enc_count, step_blocks, features, NT), lambda i, *_: (0, i, 0, 0))
    attended, partial = pl.pallas_call(
        attend_kernel,
        out_shape=(
            jax.ShapeDtypeStruct(queries.shape, bf16),
            jax.ShapeDtypeStruct((enc_count, used_count, features, NT), bf16),
        ),
        grid_spec=pltpu.PrefetchScalarGridSpec(
            num_scalar_prefetch=2,
            grid=(spans // SPANS_PER_STEP,),
            in_specs=[
                by_blocks,
                by_rows,
                by_rows,
                pl.BlockSpec((head_width, enc_features), resident),
                pl.BlockSpec((head_width, enc_features), resident),
                pl.BlockSpec((enc_features, head_width), resident),
                pl.BlockSpec((enc_features, head_width), resident),
            ],
            out_specs=[by_rows, by_blocks],
            scratch_shapes=[
                pltpu.VMEM((SPANS_PER_STEP, head_width, NBR * NT), bf16),
                pltpu.VMEM((SPANS_PER_STEP, head_width, NBR * NT), bf16),
            ],
        ),
        compiler_params=params(dimension_semantics=("arbitrary",)),
    )(
        second_valid[0],
        live_spans,
        whole,
        queries,
        cotangent,
        key_weight.T,
        value_weight.T,
        key_weight,
        value_weight,
    )

    groups = lax.all_to_all(partial, "enc", split_axis=0, concat_axis=0, tiled=True)
    by_slot = pl.pallas_call(
        merge_kernel,
        out_shape=jax.ShapeDtypeStruct((slot_total, features, NT), bf16),
        in_specs=[SMEM, VMEM],
        out_specs=VMEM,
        compiler_params=params(),
    )(slot_order, groups)
    arrived = lax.all_to_all(by_slot, "span", split_axis=0, concat_axis=0, tiled=True)
    grad_store = pl.pallas_call(
        gather_kernel,
        out_shape=jax.ShapeDtypeStruct(neighbour_store.shape, jnp.float32),
        in_specs=[SMEM, VMEM, VMEM],
        out_specs=VMEM,
        scratch_shapes=[pltpu.VMEM((blocks_here, features, NT), jnp.float32)],
        compiler_params=params(),
    )(served, arrived, scale_wide)
    return (attended, grad_store)


def solution(mesh):
    return jax.shard_map(
        per_device,
        mesh=mesh,
        in_specs=(
            P("span", "enc"),
            P("span", "enc"),
            P(None, "enc"),
            P(None, "enc"),
            P("span", None, "enc"),
            P("span", None),
            P("span", None, None),
            P("span", None),
            P("span", None),
            P("span"),
        ),
        out_specs=(P("span", "enc"), P("span", None, "enc")),
        check_vma=False,
    )
```

```python
import functools
import math

import jax
import jax.numpy as jnp
from jax import lax
from jax.experimental import pallas as pl
from jax.experimental.pallas import tpu as pltpu
from jax.sharding import PartitionSpec as P

HD = 128
CL = 64
NT = 128
NBR = 2
SPANS_PER_STEP = 2
CHUNKS = 7
MESH = pl.DeviceIdType.MESH
VMEM_BYTES = 56 * 1024 * 1024

VMEM = pl.BlockSpec(memory_space=pltpu.VMEM)
SMEM = pl.BlockSpec(memory_space=pltpu.SMEM)
ANY = pl.BlockSpec(memory_space=pl.ANY)


def params(**kw):
    return pltpu.CompilerParams(vmem_limit_bytes=VMEM_BYTES, **kw)


def pack_kernel(served_ref, store_ref, scale_ref, out_ref, encoded):
    blocks = store_ref.shape[0]

    def encode(b, carry):
        wide = store_ref[b].astype(jnp.float32)
        scaled = wide.T * scale_ref[pl.ds(b, 1), :]
        encoded[b] = scaled.astype(jnp.bfloat16)
        return carry

    lax.fori_loop(0, blocks, encode, 0)

    chunks, slots, rows, _ = out_ref.shape

    def copy(p, carry):
        b = served_ref[p]
        for c in range(chunks):
            out_ref[c, p] = encoded[b, c * rows : (c + 1) * rows]
        return carry

    lax.fori_loop(0, slots, copy, 0)


def greet(me_enc, me_span, enc_count, shard_count):
    barrier = pltpu.get_barrier_semaphore()

    def greet_span(d, carry):
        peer = lax.rem(me_span + d, shard_count)
        pl.semaphore_signal(barrier, inc=1, device_id=(me_enc, peer), device_id_type=MESH)
        return carry

    def greet_enc(d, carry):
        peer = lax.rem(me_enc + d, enc_count)
        pl.semaphore_signal(barrier, inc=1, device_id=(peer, me_span), device_id_type=MESH)
        return carry

    lax.fori_loop(1, shard_count, greet_span, 0)
    lax.fori_loop(1, enc_count, greet_enc, 0)
    pl.semaphore_wait(barrier, shard_count + enc_count - 2)


def each(count, act):
    def body(d, carry):
        act(d)
        return carry

    lax.fori_loop(1, count, body, 0)


def fetch_kernel(enc_count, shard_count, order_ref, in_ref, out_ref, *scratch):
    chunks, slots, _, _ = in_ref.shape
    capacity = slots // shard_count
    used = order_ref.shape[0]
    received, mine = scratch[:chunks], scratch[chunks : 2 * chunks]
    span_send, span_recv, span_own, enc_send, enc_recv, enc_own = scratch[2 * chunks :]
    me_enc, me_span = lax.axis_index("enc"), lax.axis_index("span")

    def span_copy(c, d):
        peer = lax.rem(me_span + d, shard_count)
        return pltpu.make_async_remote_copy(
            src_ref=in_ref.at[c, pl.ds(peer * capacity, capacity)],
            dst_ref=received[c].at[pl.ds(me_span * capacity, capacity)],
            send_sem=span_send.at[c, d],
            recv_sem=span_recv.at[c, d],
            device_id=(me_enc, peer),
            device_id_type=MESH,
        )

    def span_local(c):
        here = pl.ds(me_span * capacity, capacity)
        return pltpu.make_async_copy(in_ref.at[c, here], received[c].at[here], span_own.at[c])

    def enc_copy(c, d):
        peer = lax.rem(me_enc + d, enc_count)
        return pltpu.make_async_remote_copy(
            src_ref=mine[c],
            dst_ref=out_ref.at[c, me_enc],
            send_sem=enc_send.at[c, d],
            recv_sem=enc_recv.at[c, d],
            device_id=(peer, me_span),
            device_id_type=MESH,
        )

    def enc_local(c):
        return pltpu.make_async_copy(mine[c], out_ref.at[c, me_enc], enc_own.at[c])

    greet(me_enc, me_span, enc_count, shard_count)
    for c in range(chunks):
        each(shard_count, lambda d: span_copy(c, d).start())
        span_local(c).start()
    for c in range(chunks):
        each(shard_count, lambda d: span_copy(c, d).wait_recv())
        span_local(c).wait()

        def pick(i, carry):
            mine[c][i] = received[c][order_ref[i]]
            return carry

        lax.fori_loop(0, used, pick, 0)
        each(enc_count, lambda d: enc_copy(c, d).start())
        enc_local(c).start()
    for c in range(chunks):
        each(shard_count, lambda d: span_copy(c, d).wait_send())
        each(enc_count, lambda d: enc_copy(c, d).wait())
        enc_local(c).wait()


def return_kernel(enc_count, shard_count, place_ref, in_ref, out_ref, *scratch):
    chunks, _, used, _, _ = in_ref.shape
    slots = out_ref.shape[1]
    capacity = slots // shard_count
    groups = scratch[:chunks]
    merged = scratch[chunks : 2 * chunks]
    by_slot = scratch[2 * chunks : 3 * chunks]
    span_send, span_recv, span_own, enc_send, enc_recv, enc_own = scratch[3 * chunks :]
    me_enc, me_span = lax.axis_index("enc"), lax.axis_index("span")

    def enc_copy(c, d):
        peer = lax.rem(me_enc + d, enc_count)
        return pltpu.make_async_remote_copy(
            src_ref=in_ref.at[c, peer],
            dst_ref=groups[c].at[me_enc],
            send_sem=enc_send.at[c, d],
            recv_sem=enc_recv.at[c, d],
            device_id=(peer, me_span),
            device_id_type=MESH,
        )

    def enc_local(c):
        return pltpu.make_async_copy(in_ref.at[c, me_enc], groups[c].at[me_enc], enc_own.at[c])

    def span_copy(c, d):
        peer = lax.rem(me_span + d, shard_count)
        return pltpu.make_async_remote_copy(
            src_ref=by_slot[c].at[pl.ds(peer * capacity, capacity)],
            dst_ref=out_ref.at[c, pl.ds(me_span * capacity, capacity)],
            send_sem=span_send.at[c, d],
            recv_sem=span_recv.at[c, d],
            device_id=(me_enc, peer),
            device_id_type=MESH,
        )

    def span_local(c):
        here = pl.ds(me_span * capacity, capacity)
        return pltpu.make_async_copy(by_slot[c].at[here], out_ref.at[c, here], span_own.at[c])

    greet(me_enc, me_span, enc_count, shard_count)
    for c in range(chunks):
        each(enc_count, lambda d: enc_copy(c, d).start())
        enc_local(c).start()
    for c in range(chunks):
        each(enc_count, lambda d: enc_copy(c, d).wait_recv())
        enc_local(c).wait()
        merged[c][used] = jnp.zeros(merged[c].shape[1:], jnp.bfloat16)

        def add(i, carry):
            total = groups[c][0, i].astype(jnp.float32)
            for e in range(1, enc_count):
                total = total + groups[c][e, i].astype(jnp.float32)
            merged[c][i] = total.astype(jnp.bfloat16)
            return carry

        lax.fori_loop(0, used, add, 0)

        def put(p, carry):
            by_slot[c][p] = merged[c][place_ref[p]]
            return carry

        lax.fori_loop(0, slots, put, 0)
        each(shard_count, lambda d: span_copy(c, d).start())
        span_local(c).start()
    for c in range(chunks):
        each(enc_count, lambda d: enc_copy(c, d).wait_send())
        each(shard_count, lambda d: span_copy(c, d).wait())
        span_local(c).wait()


def attend_kernel(
    valid_ref,
    live_ref,
    x_ref,
    q_ref,
    c_ref,
    wkt_ref,
    wvt_ref,
    wk_ref,
    wv_ref,
    att_ref,
    part_ref,
    grad_k,
    grad_v,
):
    step = pl.program_id(0)
    heads = q_ref.shape[1] // HD
    chunks, enc, _, rows_c, _ = x_ref.shape
    pieces = [(e, c) for e in range(enc) for c in range(chunks)]
    scale_factor = 1.0 / math.sqrt(HD)
    cols = lax.broadcasted_iota(jnp.int32, (1, NBR * NT), 1)
    dims_t = (((0,), (0,)), ((), ()))
    dims_nt = (((1,), (1,)), ((), ()))
    f32 = jnp.float32
    for j in range(SPANS_PER_STEP):
        span = step * SPANS_PER_STEP + j
        second = valid_ref[span].astype(f32)
        live = span < live_ref[0]
        mask = jnp.where(cols < NT, 1.0, second)
        halves = [
            jnp.concatenate([x_ref[c, e, NBR * j + k] for e, c in pieces], axis=0)
            for k in range(NBR)
        ]
        x = jnp.concatenate(halves, axis=1)
        key_t = jnp.dot(wkt_ref[...], x, preferred_element_type=f32).astype(jnp.bfloat16)
        value_t = jnp.dot(wvt_ref[...], x, preferred_element_type=f32).astype(jnp.bfloat16)
        rows = slice(j * CL, (j + 1) * CL)
        for h in range(heads):
            head = slice(h * HD, (h + 1) * HD)
            q = q_ref[rows, head]
            go = c_ref[rows, head]
            go = jnp.where(live, go, jnp.zeros_like(go))
            k_t = key_t[head, :]
            v_t = value_t[head, :]
            scores = jnp.dot(q, k_t, preferred_element_type=f32) * scale_factor
            weights = jnp.exp(scores) * mask
            probs = weights / jnp.sum(weights, axis=1, keepdims=True)
            low = probs.astype(jnp.bfloat16)
            mixture = lax.dot_general(low, v_t, dims_nt, preferred_element_type=f32)
            att_ref[rows, head] = jnp.where(live, mixture, 0.0).astype(jnp.bfloat16)
            grad_v[j, head, :] = lax.dot_general(
                go, low, dims_t, preferred_element_type=f32
            ).astype(jnp.bfloat16)
            grad_p = jnp.dot(go, v_t, preferred_element_type=f32)
            inner = jnp.sum(probs * grad_p, axis=1, keepdims=True)
            grad_s = (probs * (grad_p - inner) * scale_factor).astype(jnp.bfloat16)
            grad_k[j, head, :] = lax.dot_general(
                q, grad_s, dims_t, preferred_element_type=f32
            ).astype(jnp.bfloat16)
        part = jnp.dot(wk_ref[...], grad_k[j], preferred_element_type=f32)
        part = part + jnp.dot(wv_ref[...], grad_v[j], preferred_element_type=f32)
        part = part.astype(jnp.bfloat16)
        for k in range(NBR):
            for n, (e, c) in enumerate(pieces):
                part_ref[c, e, NBR * j + k] = part[
                    n * rows_c : (n + 1) * rows_c, k * NT : (k + 1) * NT
                ]


def gather_kernel(served_ref, in_ref, scale_ref, out_ref, total):
    chunks, slots, rows, _ = in_ref.shape
    total[...] = jnp.zeros_like(total)

    def add(p, carry):
        b = served_ref[p]
        for c in range(chunks):
            here = slice(c * rows, (c + 1) * rows)
            total[b, here] = total[b, here] + in_ref[c, p].astype(jnp.float32)
        return carry

    lax.fori_loop(0, slots, add, 0)

    def write(b, carry):
        scaled = total[b] * scale_ref[pl.ds(b, 1), :]
        out_ref[b] = scaled.T
        return carry

    lax.fori_loop(0, out_ref.shape[0], write, 0)


def per_device(
    queries,
    cotangent,
    key_weight,
    value_weight,
    neighbour_store,
    block_scale,
    fetch_index,
    neighbour_slot,
    second_valid,
    live_spans,
):
    enc_count = lax.axis_size("enc")
    shard_count = lax.axis_size("span")
    slot_total = shard_count * fetch_index.shape[2]
    blocks_here, _, features = neighbour_store.shape
    enc_features, head_width = key_weight.shape
    slot_order = neighbour_slot[0]
    used_count = slot_order.shape[0]
    spans = used_count // NBR
    served = fetch_index[0].reshape(slot_total)
    scale_wide = block_scale.astype(jnp.float32)
    bf16 = jnp.bfloat16
    rows = features // CHUNKS
    used_index = jnp.arange(used_count, dtype=jnp.int32)
    slot_index = jnp.arange(slot_total, dtype=jnp.int32)
    named = slot_order[None, :] == slot_index[:, None]
    place = jnp.min(jnp.where(named, used_index[None, :], used_count), axis=1)

    outgoing = pl.pallas_call(
        pack_kernel,
        out_shape=jax.ShapeDtypeStruct((CHUNKS, slot_total, rows, NT), bf16),
        in_specs=[SMEM, VMEM, VMEM],
        out_specs=VMEM,
        scratch_shapes=[pltpu.VMEM((blocks_here, features, NT), bf16)],
        compiler_params=params(),
    )(served, neighbour_store, scale_wide)
    dma = pltpu.SemaphoreType.DMA
    semaphores = [
        dma((CHUNKS, shard_count)),
        dma((CHUNKS, shard_count)),
        dma((CHUNKS,)),
        dma((CHUNKS, enc_count)),
        dma((CHUNKS, enc_count)),
        dma((CHUNKS,)),
    ]
    whole = pl.pallas_call(
        functools.partial(fetch_kernel, enc_count, shard_count),
        out_shape=jax.ShapeDtypeStruct((CHUNKS, enc_count, used_count, rows, NT), bf16),
        in_specs=[SMEM, VMEM],
        out_specs=ANY,
        scratch_shapes=[pltpu.VMEM((slot_total, rows, NT), bf16)] * CHUNKS
        + [pltpu.VMEM((used_count, rows, NT), bf16)] * CHUNKS
        + semaphores,
        compiler_params=params(collective_id=0, has_side_effects=True),
    )(slot_order, outgoing)

    step_blocks = SPANS_PER_STEP * NBR
    step_rows = SPANS_PER_STEP * CL
    resident = lambda i, *_: (0, 0)
    by_rows = pl.BlockSpec((step_rows, head_width), lambda i, *_: (i, 0))
    by_blocks = pl.BlockSpec(
        (CHUNKS, enc_count, step_blocks, rows, NT), lambda i, *_: (0, 0, i, 0, 0)
    )
    attended, partial = pl.pallas_call(
        attend_kernel,
        out_shape=(
            jax.ShapeDtypeStruct(queries.shape, bf16),
            jax.ShapeDtypeStruct(whole.shape, bf16),
        ),
        grid_spec=pltpu.PrefetchScalarGridSpec(
            num_scalar_prefetch=2,
            grid=(spans // SPANS_PER_STEP,),
            in_specs=[
                by_blocks,
                by_rows,
                by_rows,
                pl.BlockSpec((head_width, enc_features), resident),
                pl.BlockSpec((head_width, enc_features), resident),
                pl.BlockSpec((enc_features, head_width), resident),
                pl.BlockSpec((enc_features, head_width), resident),
            ],
            out_specs=[by_rows, by_blocks],
            scratch_shapes=[
                pltpu.VMEM((SPANS_PER_STEP, head_width, NBR * NT), bf16),
                pltpu.VMEM((SPANS_PER_STEP, head_width, NBR * NT), bf16),
            ],
        ),
        compiler_params=params(dimension_semantics=("arbitrary",)),
    )(
        second_valid[0],
        live_spans,
        whole,
        queries,
        cotangent,
        key_weight.T,
        value_weight.T,
        key_weight,
        value_weight,
    )

    arrived = pl.pallas_call(
        functools.partial(return_kernel, enc_count, shard_count),
        out_shape=jax.ShapeDtypeStruct((CHUNKS, slot_total, rows, NT), bf16),
        in_specs=[SMEM, ANY],
        out_specs=ANY,
        scratch_shapes=[pltpu.VMEM((enc_count, used_count, rows, NT), bf16)] * CHUNKS
        + [pltpu.VMEM((used_count + 1, rows, NT), bf16)] * CHUNKS
        + [pltpu.VMEM((slot_total, rows, NT), bf16)] * CHUNKS
        + semaphores,
        compiler_params=params(collective_id=1, has_side_effects=True),
    )(place, partial)
    grad_store = pl.pallas_call(
        gather_kernel,
        out_shape=jax.ShapeDtypeStruct(neighbour_store.shape, jnp.float32),
        in_specs=[SMEM, VMEM, VMEM],
        out_specs=VMEM,
        scratch_shapes=[pltpu.VMEM((blocks_here, features, NT), jnp.float32)],
        compiler_params=params(),
    )(served, arrived, scale_wide)
    return (attended, grad_store)


def solution(mesh):
    return jax.shard_map(
        per_device,
        mesh=mesh,
        in_specs=(
            P("span", "enc"),
            P("span", "enc"),
            P(None, "enc"),
            P(None, "enc"),
            P("span", None, "enc"),
            P("span", None),
            P("span", None, None),
            P("span", None),
            P("span", None),
            P("span"),
        ),
        out_specs=(P("span", "enc"), P("span", None, "enc")),
        check_vma=False,
    )
```

```python
import functools
import math

import jax
import jax.numpy as jnp
from jax import lax
from jax.experimental import pallas as pl
from jax.experimental.pallas import tpu as pltpu
from jax.sharding import PartitionSpec as P

HD = 128
CL = 64
NT = 128
NBR = 2
SPANS_PER_STEP = 2
SPANS_TOGETHER = 1
CHUNKS = 7
WINDOW = 1
MESH = pl.DeviceIdType.MESH
VMEM_BYTES = 56 * 1024 * 1024

VMEM = pl.BlockSpec(memory_space=pltpu.VMEM)
SMEM = pl.BlockSpec(memory_space=pltpu.SMEM)
ANY = pl.BlockSpec(memory_space=pl.ANY)


def params(**kw):
    return pltpu.CompilerParams(vmem_limit_bytes=VMEM_BYTES, **kw)


def greet(me_enc, me_span, enc_count, shard_count):
    barrier = pltpu.get_barrier_semaphore()

    def greet_span(d, carry):
        peer = lax.rem(me_span + d, shard_count)
        pl.semaphore_signal(barrier, inc=1, device_id=(me_enc, peer), device_id_type=MESH)
        return carry

    def greet_enc(d, carry):
        peer = lax.rem(me_enc + d, enc_count)
        pl.semaphore_signal(barrier, inc=1, device_id=(peer, me_span), device_id_type=MESH)
        return carry

    lax.fori_loop(1, shard_count, greet_span, 0)
    lax.fori_loop(1, enc_count, greet_enc, 0)
    pl.semaphore_wait(barrier, shard_count + enc_count - 2)


def each(count, act):
    def body(d, carry):
        act(d)
        return carry

    lax.fori_loop(1, count, body, 0)


def fetch_kernel(
    enc_count, shard_count, order_ref, served_ref, store_ref, scale_ref, out_ref, *scratch
):
    chunks, _, used, rows, _ = out_ref.shape
    slots = served_ref.shape[0]
    capacity = slots // shard_count
    outgoing, received = scratch[:chunks], scratch[chunks : 2 * chunks]
    mine = scratch[2 * chunks : 3 * chunks]
    span_send, span_recv, span_own, enc_send, enc_recv, enc_own = scratch[3 * chunks :]
    me_enc, me_span = lax.axis_index("enc"), lax.axis_index("span")

    def span_copy(c, d):
        peer = lax.rem(me_span + d, shard_count)
        return pltpu.make_async_remote_copy(
            src_ref=outgoing[c].at[pl.ds(peer * capacity, capacity)],
            dst_ref=received[c].at[pl.ds(me_span * capacity, capacity)],
            send_sem=span_send.at[c, d],
            recv_sem=span_recv.at[c, d],
            device_id=(me_enc, peer),
            device_id_type=MESH,
        )

    def span_local(c):
        here = pl.ds(me_span * capacity, capacity)
        return pltpu.make_async_copy(outgoing[c].at[here], received[c].at[here], span_own.at[c])

    def enc_copy(c, d):
        peer = lax.rem(me_enc + d, enc_count)
        return pltpu.make_async_remote_copy(
            src_ref=mine[c],
            dst_ref=out_ref.at[c, me_enc],
            send_sem=enc_send.at[c, d],
            recv_sem=enc_recv.at[c, d],
            device_id=(peer, me_span),
            device_id_type=MESH,
        )

    def enc_local(c):
        return pltpu.make_async_copy(mine[c], out_ref.at[c, me_enc], enc_own.at[c])

    def pack(c):
        def encode(p, carry):
            b = served_ref[p]
            wide = store_ref[b, c * rows : (c + 1) * rows].astype(jnp.float32)
            outgoing[c][p] = (wide * scale_ref[b]).astype(jnp.bfloat16)
            return carry

        lax.fori_loop(0, slots, encode, 0, unroll=4)

    def send(c):
        each(shard_count, lambda d: span_copy(c, d).start())
        span_local(c).start()

    pack(0)
    greet(me_enc, me_span, enc_count, shard_count)
    send(0)
    for c in range(1, chunks):
        pack(c)
        if c < WINDOW:
            send(c)
    for c in range(chunks):
        each(shard_count, lambda d: span_copy(c, d).wait_recv())
        span_local(c).wait()
        if c + WINDOW < chunks:
            send(c + WINDOW)

        def pick(i, carry):
            mine[c][i] = received[c][order_ref[i]]
            return carry

        lax.fori_loop(0, used, pick, 0, unroll=4)
        each(enc_count, lambda d: enc_copy(c, d).start())
        enc_local(c).start()
    for c in range(chunks):
        each(shard_count, lambda d: span_copy(c, d).wait_send())
        each(enc_count, lambda d: enc_copy(c, d).wait())
        enc_local(c).wait()


def return_kernel(enc_count, shard_count, place_ref, in_ref, out_ref, *scratch):
    chunks, _, used, _, _ = in_ref.shape
    slots = out_ref.shape[1]
    capacity = slots // shard_count
    groups = scratch[:chunks]
    merged = scratch[chunks : 2 * chunks]
    by_slot = scratch[2 * chunks : 3 * chunks]
    span_send, span_recv, span_own, enc_send, enc_recv, enc_own = scratch[3 * chunks :]
    me_enc, me_span = lax.axis_index("enc"), lax.axis_index("span")

    def enc_copy(c, d):
        peer = lax.rem(me_enc + d, enc_count)
        return pltpu.make_async_remote_copy(
            src_ref=in_ref.at[c, peer],
            dst_ref=groups[c].at[me_enc],
            send_sem=enc_send.at[c, d],
            recv_sem=enc_recv.at[c, d],
            device_id=(peer, me_span),
            device_id_type=MESH,
        )

    def enc_local(c):
        return pltpu.make_async_copy(in_ref.at[c, me_enc], groups[c].at[me_enc], enc_own.at[c])

    def span_copy(c, d):
        peer = lax.rem(me_span + d, shard_count)
        return pltpu.make_async_remote_copy(
            src_ref=by_slot[c].at[pl.ds(peer * capacity, capacity)],
            dst_ref=out_ref.at[c, pl.ds(me_span * capacity, capacity)],
            send_sem=span_send.at[c, d],
            recv_sem=span_recv.at[c, d],
            device_id=(me_enc, peer),
            device_id_type=MESH,
        )

    def span_local(c):
        here = pl.ds(me_span * capacity, capacity)
        return pltpu.make_async_copy(by_slot[c].at[here], out_ref.at[c, here], span_own.at[c])

    greet(me_enc, me_span, enc_count, shard_count)
    for c in range(chunks):
        each(enc_count, lambda d: enc_copy(c, d).start())
        enc_local(c).start()
    for c in range(chunks):
        each(enc_count, lambda d: enc_copy(c, d).wait_recv())
        enc_local(c).wait()
        merged[c][used] = jnp.zeros(merged[c].shape[1:], jnp.bfloat16)

        def add(i, carry):
            total = groups[c][0, i].astype(jnp.float32)
            for e in range(1, enc_count):
                total = total + groups[c][e, i].astype(jnp.float32)
            merged[c][i] = total.astype(jnp.bfloat16)
            return carry

        lax.fori_loop(0, used, add, 0, unroll=4)

        def put(p, carry):
            by_slot[c][p] = merged[c][place_ref[p]]
            return carry

        lax.fori_loop(0, slots, put, 0, unroll=4)
        each(shard_count, lambda d: span_copy(c, d).start())
        span_local(c).start()
    for c in range(chunks):
        each(enc_count, lambda d: enc_copy(c, d).wait_send())
        each(shard_count, lambda d: span_copy(c, d).wait())
        span_local(c).wait()


def attend_kernel(
    valid_ref,
    live_ref,
    x_ref,
    q_ref,
    c_ref,
    wkt_ref,
    wvt_ref,
    wk_ref,
    wv_ref,
    att_ref,
    part_ref,
    key_t,
    value_t,
    grad_k,
    grad_v,
):
    step = pl.program_id(0)
    heads = q_ref.shape[1] // HD
    chunks, enc, _, rows_c, _ = x_ref.shape
    pieces = [(e, c) for e in range(enc) for c in range(chunks)]
    scale_factor = 1.0 / math.sqrt(HD)
    cols = lax.broadcasted_iota(jnp.int32, (1, NBR * NT), 1)
    dims_t = (((0,), (0,)), ((), ()))
    dims_nt = (((1,), (1,)), ((), ()))
    f32 = jnp.float32
    bf16 = jnp.bfloat16
    lives, masks, xs = [], [], []
    for j in range(SPANS_PER_STEP):
        span = step * SPANS_PER_STEP + j
        second = valid_ref[span].astype(f32)
        lives.append(span < live_ref[0])
        masks.append(jnp.where(cols < NT, 1.0, second))
        for k in range(NBR):
            xs.append(jnp.concatenate([x_ref[c, e, NBR * j + k] for e, c in pieces], axis=0))
    x = jnp.concatenate(xs, axis=1)
    key_t[...] = jnp.dot(wkt_ref[...], x, preferred_element_type=f32).astype(bf16)
    value_t[...] = jnp.dot(wvt_ref[...], x, preferred_element_type=f32).astype(bf16)

    for j0 in range(0, SPANS_PER_STEP, SPANS_TOGETHER):
        items = []
        for j in range(j0, j0 + SPANS_TOGETHER):
            for h in range(heads):
                rows = slice(j * CL, (j + 1) * CL)
                keys = slice(j * NBR * NT, (j + 1) * NBR * NT)
                items.append((j, rows, slice(h * HD, (h + 1) * HD), keys))
        scores = [
            jnp.dot(q_ref[rows, head], key_t[head, keys], preferred_element_type=f32)
            for j, rows, head, keys in items
        ]
        grad_out = [
            jnp.where(lives[j], c_ref[rows, head], jnp.zeros((CL, HD), bf16))
            for j, rows, head, keys in items
        ]
        grad_p = [
            jnp.dot(go, value_t[head, keys], preferred_element_type=f32)
            for go, (j, rows, head, keys) in zip(grad_out, items)
        ]
        probs = []
        for raw, (j, rows, head, keys) in zip(scores, items):
            weights = jnp.exp(raw * scale_factor) * masks[j]
            probs.append(weights / jnp.sum(weights, axis=1, keepdims=True))
        low = [p.astype(bf16) for p in probs]
        grad_s = []
        for p, gp in zip(probs, grad_p):
            inner = jnp.sum(p * gp, axis=1, keepdims=True)
            grad_s.append((p * (gp - inner) * scale_factor).astype(bf16))
        for pl_low, (j, rows, head, keys) in zip(low, items):
            mixture = lax.dot_general(
                pl_low, value_t[head, keys], dims_nt, preferred_element_type=f32
            )
            att_ref[rows, head] = jnp.where(lives[j], mixture, 0.0).astype(bf16)
        for go, pl_low, (j, rows, head, keys) in zip(grad_out, low, items):
            grad_v[head, keys] = lax.dot_general(
                go, pl_low, dims_t, preferred_element_type=f32
            ).astype(bf16)
        for gs, (j, rows, head, keys) in zip(grad_s, items):
            grad_k[head, keys] = lax.dot_general(
                q_ref[rows, head], gs, dims_t, preferred_element_type=f32
            ).astype(bf16)

    part = jnp.dot(wk_ref[...], grad_k[...], preferred_element_type=f32)
    part = part + jnp.dot(wv_ref[...], grad_v[...], preferred_element_type=f32)
    part = part.astype(bf16)
    for b in range(SPANS_PER_STEP * NBR):
        for n, (e, c) in enumerate(pieces):
            part_ref[c, e, b] = part[n * rows_c : (n + 1) * rows_c, b * NT : (b + 1) * NT]


def gather_kernel(served_ref, in_ref, scale_ref, out_ref, total):
    chunks, slots, rows, _ = in_ref.shape
    total[...] = jnp.zeros_like(total)

    def add(p, carry):
        b = served_ref[p]
        for c in range(chunks):
            here = slice(c * rows, (c + 1) * rows)
            total[b, here] = total[b, here] + in_ref[c, p].astype(jnp.float32)
        return carry

    lax.fori_loop(0, slots, add, 0)

    def write(b, carry):
        out_ref[b] = total[b] * scale_ref[b]
        return carry

    lax.fori_loop(0, out_ref.shape[0], write, 0)


def per_device(
    queries,
    cotangent,
    key_weight,
    value_weight,
    neighbour_store,
    block_scale,
    fetch_index,
    neighbour_slot,
    second_valid,
    live_spans,
):
    enc_count = lax.axis_size("enc")
    shard_count = lax.axis_size("span")
    slot_total = shard_count * fetch_index.shape[2]
    blocks_here, _, features = neighbour_store.shape
    enc_features, head_width = key_weight.shape
    slot_order = neighbour_slot[0]
    used_count = slot_order.shape[0]
    spans = used_count // NBR
    served = fetch_index[0].reshape(slot_total)
    scale_wide = block_scale.astype(jnp.float32)[:, None, :]
    store_rows = neighbour_store.transpose(0, 2, 1)
    bf16 = jnp.bfloat16
    rows = features // CHUNKS
    used_index = jnp.arange(used_count, dtype=jnp.int32)
    slot_index = jnp.arange(slot_total, dtype=jnp.int32)
    named = slot_order[None, :] == slot_index[:, None]
    place = jnp.min(jnp.where(named, used_index[None, :], used_count), axis=1)

    dma = pltpu.SemaphoreType.DMA
    semaphores = [
        dma((CHUNKS, shard_count)),
        dma((CHUNKS, shard_count)),
        dma((CHUNKS,)),
        dma((CHUNKS, enc_count)),
        dma((CHUNKS, enc_count)),
        dma((CHUNKS,)),
    ]
    whole = pl.pallas_call(
        functools.partial(fetch_kernel, enc_count, shard_count),
        out_shape=jax.ShapeDtypeStruct((CHUNKS, enc_count, used_count, rows, NT), bf16),
        in_specs=[SMEM, SMEM, VMEM, VMEM],
        out_specs=ANY,
        scratch_shapes=[pltpu.VMEM((slot_total, rows, NT), bf16)] * (2 * CHUNKS)
        + [pltpu.VMEM((used_count, rows, NT), bf16)] * CHUNKS
        + semaphores,
        compiler_params=params(collective_id=0, has_side_effects=True),
    )(slot_order, served, store_rows, scale_wide)

    step_blocks = SPANS_PER_STEP * NBR
    step_rows = SPANS_PER_STEP * CL
    resident = lambda i, *_: (0, 0)
    by_rows = pl.BlockSpec((step_rows, head_width), lambda i, *_: (i, 0))
    by_blocks = pl.BlockSpec(
        (CHUNKS, enc_count, step_blocks, rows, NT), lambda i, *_: (0, 0, i, 0, 0)
    )
    attended, partial = pl.pallas_call(
        attend_kernel,
        out_shape=(
            jax.ShapeDtypeStruct(queries.shape, bf16),
            jax.ShapeDtypeStruct(whole.shape, bf16),
        ),
        grid_spec=pltpu.PrefetchScalarGridSpec(
            num_scalar_prefetch=2,
            grid=(spans // SPANS_PER_STEP,),
            in_specs=[
                by_blocks,
                by_rows,
                by_rows,
                pl.BlockSpec((head_width, enc_features), resident),
                pl.BlockSpec((head_width, enc_features), resident),
                pl.BlockSpec((enc_features, head_width), resident),
                pl.BlockSpec((enc_features, head_width), resident),
            ],
            out_specs=[by_rows, by_blocks],
            scratch_shapes=[
                pltpu.VMEM((head_width, step_blocks * NT), bf16),
            ]
            * 4,
        ),
        compiler_params=params(dimension_semantics=("arbitrary",)),
    )(
        second_valid[0],
        live_spans,
        whole,
        queries,
        cotangent,
        key_weight.T,
        value_weight.T,
        key_weight,
        value_weight,
    )

    arrived = pl.pallas_call(
        functools.partial(return_kernel, enc_count, shard_count),
        out_shape=jax.ShapeDtypeStruct((CHUNKS, slot_total, rows, NT), bf16),
        in_specs=[SMEM, ANY],
        out_specs=ANY,
        scratch_shapes=[pltpu.VMEM((enc_count, used_count, rows, NT), bf16)] * CHUNKS
        + [pltpu.VMEM((used_count + 1, rows, NT), bf16)] * CHUNKS
        + [pltpu.VMEM((slot_total, rows, NT), bf16)] * CHUNKS
        + semaphores,
        compiler_params=params(collective_id=1, has_side_effects=True),
    )(place, partial)
    grad_store = pl.pallas_call(
        gather_kernel,
        out_shape=jax.ShapeDtypeStruct(store_rows.shape, jnp.float32),
        in_specs=[SMEM, VMEM, VMEM],
        out_specs=VMEM,
        scratch_shapes=[pltpu.VMEM((blocks_here, features, NT), jnp.float32)],
        compiler_params=params(),
    )(served, arrived, scale_wide)
    return (attended, grad_store.transpose(0, 2, 1))


def solution(mesh):
    return jax.shard_map(
        per_device,
        mesh=mesh,
        in_specs=(
            P("span", "enc"),
            P("span", "enc"),
            P(None, "enc"),
            P(None, "enc"),
            P("span", None, "enc"),
            P("span", None),
            P("span", None, None),
            P("span", None),
            P("span", None),
            P("span"),
        ),
        out_specs=(P("span", "enc"), P("span", None, "enc")),
        check_vma=False,
    )
```

```python
import functools
import math

import jax
import jax.numpy as jnp
from jax import lax
from jax.experimental import pallas as pl
from jax.experimental.pallas import tpu as pltpu
from jax.sharding import PartitionSpec as P

HD = 128
CL = 64
NT = 128
NBR = 2
SPANS_PER_STEP = 2
SPANS_TOGETHER = 2
CHUNKS = 14
WINDOW = 2
ENC_WINDOW = 2
MESH = pl.DeviceIdType.MESH
VMEM_BYTES = 56 * 1024 * 1024

VMEM = pl.BlockSpec(memory_space=pltpu.VMEM)
SMEM = pl.BlockSpec(memory_space=pltpu.SMEM)
ANY = pl.BlockSpec(memory_space=pl.ANY)


def params(**kw):
    return pltpu.CompilerParams(vmem_limit_bytes=VMEM_BYTES, **kw)


def greet(me_enc, me_span, enc_count, shard_count):
    barrier = pltpu.get_barrier_semaphore()

    def greet_span(d, carry):
        peer = lax.rem(me_span + d, shard_count)
        pl.semaphore_signal(barrier, inc=1, device_id=(me_enc, peer), device_id_type=MESH)
        return carry

    def greet_enc(d, carry):
        peer = lax.rem(me_enc + d, enc_count)
        pl.semaphore_signal(barrier, inc=1, device_id=(peer, me_span), device_id_type=MESH)
        return carry

    lax.fori_loop(1, shard_count, greet_span, 0)
    lax.fori_loop(1, enc_count, greet_enc, 0)
    pl.semaphore_wait(barrier, shard_count + enc_count - 2)


def each(count, act):
    def body(d, carry):
        act(d)
        return carry

    lax.fori_loop(1, count, body, 0)


def fetch_kernel(
    enc_count, shard_count, order_ref, served_ref, store_ref, scale_ref, out_ref, *scratch
):
    chunks, _, used, rows, _ = out_ref.shape
    slots = served_ref.shape[0]
    capacity = slots // shard_count
    outgoing, received = scratch[:chunks], scratch[chunks : 2 * chunks]
    mine = scratch[2 * chunks : 3 * chunks]
    span_send, span_recv, span_own, enc_send, enc_recv, enc_own = scratch[3 * chunks :]
    me_enc, me_span = lax.axis_index("enc"), lax.axis_index("span")

    def span_copy(c, d):
        peer = lax.rem(me_span + d, shard_count)
        return pltpu.make_async_remote_copy(
            src_ref=outgoing[c].at[pl.ds(peer * capacity, capacity)],
            dst_ref=received[c].at[pl.ds(me_span * capacity, capacity)],
            send_sem=span_send.at[c, d],
            recv_sem=span_recv.at[c, d],
            device_id=(me_enc, peer),
            device_id_type=MESH,
        )

    def span_local(c):
        here = pl.ds(me_span * capacity, capacity)
        return pltpu.make_async_copy(outgoing[c].at[here], received[c].at[here], span_own.at[c])

    def enc_copy(c, d):
        peer = lax.rem(me_enc + d, enc_count)
        return pltpu.make_async_remote_copy(
            src_ref=mine[c],
            dst_ref=out_ref.at[c, me_enc],
            send_sem=enc_send.at[c, d],
            recv_sem=enc_recv.at[c, d],
            device_id=(peer, me_span),
            device_id_type=MESH,
        )

    def enc_local(c):
        return pltpu.make_async_copy(mine[c], out_ref.at[c, me_enc], enc_own.at[c])

    def pack(c):
        def encode(p, carry):
            b = served_ref[p]
            wide = store_ref[b, c * rows : (c + 1) * rows].astype(jnp.float32)
            outgoing[c][p] = (wide * scale_ref[b]).astype(jnp.bfloat16)
            return carry

        lax.fori_loop(0, slots, encode, 0, unroll=4)

    def send(c):
        each(shard_count, lambda d: span_copy(c, d).start())
        span_local(c).start()

    pack(0)
    greet(me_enc, me_span, enc_count, shard_count)
    send(0)
    for c in range(1, chunks):
        pack(c)
        if c < WINDOW:
            send(c)
    for c in range(chunks):
        each(shard_count, lambda d: span_copy(c, d).wait_recv())
        span_local(c).wait()
        if c + WINDOW < chunks:
            send(c + WINDOW)

        def pick(i, carry):
            mine[c][i] = received[c][order_ref[i]]
            return carry

        lax.fori_loop(0, used, pick, 0, unroll=4)
        each(enc_count, lambda d: enc_copy(c, d).start())
        enc_local(c).start()
    for c in range(chunks):
        each(shard_count, lambda d: span_copy(c, d).wait_send())
        each(enc_count, lambda d: enc_copy(c, d).wait())
        enc_local(c).wait()


def return_kernel(enc_count, shard_count, place_ref, in_ref, out_ref, *scratch):
    chunks, _, used, _, _ = in_ref.shape
    slots = out_ref.shape[1]
    capacity = slots // shard_count
    groups = scratch[:chunks]
    merged = scratch[chunks : 2 * chunks]
    by_slot = scratch[2 * chunks : 3 * chunks]
    span_send, span_recv, span_own, enc_send, enc_recv, enc_own = scratch[3 * chunks :]
    me_enc, me_span = lax.axis_index("enc"), lax.axis_index("span")

    def enc_copy(c, d):
        peer = lax.rem(me_enc + d, enc_count)
        return pltpu.make_async_remote_copy(
            src_ref=in_ref.at[c, peer],
            dst_ref=groups[c].at[me_enc],
            send_sem=enc_send.at[c, d],
            recv_sem=enc_recv.at[c, d],
            device_id=(peer, me_span),
            device_id_type=MESH,
        )

    def enc_local(c):
        return pltpu.make_async_copy(in_ref.at[c, me_enc], groups[c].at[me_enc], enc_own.at[c])

    def span_copy(c, d):
        peer = lax.rem(me_span + d, shard_count)
        return pltpu.make_async_remote_copy(
            src_ref=by_slot[c].at[pl.ds(peer * capacity, capacity)],
            dst_ref=out_ref.at[c, pl.ds(me_span * capacity, capacity)],
            send_sem=span_send.at[c, d],
            recv_sem=span_recv.at[c, d],
            device_id=(me_enc, peer),
            device_id_type=MESH,
        )

    def span_local(c):
        here = pl.ds(me_span * capacity, capacity)
        return pltpu.make_async_copy(by_slot[c].at[here], out_ref.at[c, here], span_own.at[c])

    greet(me_enc, me_span, enc_count, shard_count)

    def send(c):
        each(enc_count, lambda d: enc_copy(c, d).start())
        enc_local(c).start()

    for c in range(min(ENC_WINDOW, chunks)):
        send(c)
    for c in range(chunks):
        each(enc_count, lambda d: enc_copy(c, d).wait_recv())
        enc_local(c).wait()
        if c + ENC_WINDOW < chunks:
            send(c + ENC_WINDOW)
        merged[c][used] = jnp.zeros(merged[c].shape[1:], jnp.bfloat16)

        def add(i, carry):
            total = groups[c][0, i].astype(jnp.float32)
            for e in range(1, enc_count):
                total = total + groups[c][e, i].astype(jnp.float32)
            merged[c][i] = total.astype(jnp.bfloat16)
            return carry

        lax.fori_loop(0, used, add, 0, unroll=4)

        def put(p, carry):
            by_slot[c][p] = merged[c][place_ref[p]]
            return carry

        lax.fori_loop(0, slots, put, 0, unroll=4)
        each(shard_count, lambda d: span_copy(c, d).start())
        span_local(c).start()
    for c in range(chunks):
        each(enc_count, lambda d: enc_copy(c, d).wait_send())
        each(shard_count, lambda d: span_copy(c, d).wait())
        span_local(c).wait()


def attend_kernel(
    valid_ref,
    live_ref,
    x_ref,
    q_ref,
    c_ref,
    wk_ref,
    wv_ref,
    att_ref,
    part_ref,
    key_t,
    value_t,
    grad_k,
    grad_v,
    wkt_ref,
    wvt_ref,
):
    step = pl.program_id(0)
    heads = q_ref.shape[1] // HD
    chunks, enc, _, rows_c, _ = x_ref.shape
    pieces = [(e, c) for e in range(enc) for c in range(chunks)]
    scale_factor = 1.0 / math.sqrt(HD)
    cols = lax.broadcasted_iota(jnp.int32, (1, NBR * NT), 1)
    dims_t = (((0,), (0,)), ((), ()))
    dims_nt = (((1,), (1,)), ((), ()))
    f32 = jnp.float32
    bf16 = jnp.bfloat16

    @pl.when(step == 0)
    def _():
        wkt_ref[...] = wk_ref[...].T
        wvt_ref[...] = wv_ref[...].T

    lives, masks, xs = [], [], []
    for j in range(SPANS_PER_STEP):
        span = step * SPANS_PER_STEP + j
        second = valid_ref[span].astype(f32)
        lives.append(span < live_ref[0])
        masks.append(jnp.where(cols < NT, 1.0, second))
        for k in range(NBR):
            xs.append(jnp.concatenate([x_ref[c, e, NBR * j + k] for e, c in pieces], axis=0))
    x = jnp.concatenate(xs, axis=1)
    key_t[...] = jnp.dot(wkt_ref[...], x, preferred_element_type=f32).astype(bf16)
    value_t[...] = jnp.dot(wvt_ref[...], x, preferred_element_type=f32).astype(bf16)

    for j0 in range(0, SPANS_PER_STEP, SPANS_TOGETHER):
        items = []
        for j in range(j0, j0 + SPANS_TOGETHER):
            for h in range(heads):
                rows = slice(j * CL, (j + 1) * CL)
                keys = slice(j * NBR * NT, (j + 1) * NBR * NT)
                items.append((j, rows, slice(h * HD, (h + 1) * HD), keys))
        scores = [
            jnp.dot(q_ref[rows, head], key_t[head, keys], preferred_element_type=f32)
            for j, rows, head, keys in items
        ]
        grad_out = [
            jnp.where(lives[j], c_ref[rows, head], jnp.zeros((CL, HD), bf16))
            for j, rows, head, keys in items
        ]
        grad_p = [
            jnp.dot(go, value_t[head, keys], preferred_element_type=f32)
            for go, (j, rows, head, keys) in zip(grad_out, items)
        ]
        probs = []
        for raw, (j, rows, head, keys) in zip(scores, items):
            weights = jnp.exp(raw * scale_factor) * masks[j]
            probs.append(weights / jnp.sum(weights, axis=1, keepdims=True))
        low = [p.astype(bf16) for p in probs]
        grad_s = []
        for p, gp in zip(probs, grad_p):
            inner = jnp.sum(p * gp, axis=1, keepdims=True)
            grad_s.append((p * (gp - inner) * scale_factor).astype(bf16))
        for pl_low, (j, rows, head, keys) in zip(low, items):
            mixture = lax.dot_general(
                pl_low, value_t[head, keys], dims_nt, preferred_element_type=f32
            )
            att_ref[rows, head] = jnp.where(lives[j], mixture, 0.0).astype(bf16)
        for go, pl_low, (j, rows, head, keys) in zip(grad_out, low, items):
            grad_v[head, keys] = lax.dot_general(
                go, pl_low, dims_t, preferred_element_type=f32
            ).astype(bf16)
        for gs, (j, rows, head, keys) in zip(grad_s, items):
            grad_k[head, keys] = lax.dot_general(
                q_ref[rows, head], gs, dims_t, preferred_element_type=f32
            ).astype(bf16)

    part = jnp.dot(wk_ref[...], grad_k[...], preferred_element_type=f32)
    part = part + jnp.dot(wv_ref[...], grad_v[...], preferred_element_type=f32)
    part = part.astype(bf16)
    for b in range(SPANS_PER_STEP * NBR):
        for n, (e, c) in enumerate(pieces):
            part_ref[c, e, b] = part[n * rows_c : (n + 1) * rows_c, b * NT : (b + 1) * NT]


def gather_kernel(served_ref, in_ref, scale_ref, out_ref, total):
    chunks, slots, rows, _ = in_ref.shape
    total[...] = jnp.zeros_like(total)

    def add(p, carry):
        b = served_ref[p]
        for c in range(chunks):
            here = slice(c * rows, (c + 1) * rows)
            total[b, here] = total[b, here] + in_ref[c, p].astype(jnp.float32)
        return carry

    lax.fori_loop(0, slots, add, 0)

    def write(b, carry):
        out_ref[b] = total[b] * scale_ref[b]
        return carry

    lax.fori_loop(0, out_ref.shape[0], write, 0)


def per_device(
    queries,
    cotangent,
    key_weight,
    value_weight,
    neighbour_store,
    block_scale,
    fetch_index,
    neighbour_slot,
    second_valid,
    live_spans,
):
    enc_count = lax.axis_size("enc")
    shard_count = lax.axis_size("span")
    slot_total = shard_count * fetch_index.shape[2]
    blocks_here, _, features = neighbour_store.shape
    enc_features, head_width = key_weight.shape
    slot_order = neighbour_slot[0]
    used_count = slot_order.shape[0]
    spans = used_count // NBR
    served = fetch_index[0].reshape(slot_total)
    scale_wide = block_scale.astype(jnp.float32)[:, None, :]
    store_rows = neighbour_store.transpose(0, 2, 1)
    bf16 = jnp.bfloat16
    rows = features // CHUNKS
    used_index = jnp.arange(used_count, dtype=jnp.int32)
    slot_index = jnp.arange(slot_total, dtype=jnp.int32)
    named = slot_order[None, :] == slot_index[:, None]
    place = jnp.min(jnp.where(named, used_index[None, :], used_count), axis=1)

    dma = pltpu.SemaphoreType.DMA
    semaphores = [
        dma((CHUNKS, shard_count)),
        dma((CHUNKS, shard_count)),
        dma((CHUNKS,)),
        dma((CHUNKS, enc_count)),
        dma((CHUNKS, enc_count)),
        dma((CHUNKS,)),
    ]
    whole = pl.pallas_call(
        functools.partial(fetch_kernel, enc_count, shard_count),
        out_shape=jax.ShapeDtypeStruct((CHUNKS, enc_count, used_count, rows, NT), bf16),
        in_specs=[SMEM, SMEM, VMEM, VMEM],
        out_specs=ANY,
        scratch_shapes=[pltpu.VMEM((slot_total, rows, NT), bf16)] * (2 * CHUNKS)
        + [pltpu.VMEM((used_count, rows, NT), bf16)] * CHUNKS
        + semaphores,
        compiler_params=params(collective_id=0, has_side_effects=True),
    )(slot_order, served, store_rows, scale_wide)

    step_blocks = SPANS_PER_STEP * NBR
    step_rows = SPANS_PER_STEP * CL
    resident = lambda i, *_: (0, 0)
    by_rows = pl.BlockSpec((step_rows, head_width), lambda i, *_: (i, 0))
    by_blocks = pl.BlockSpec(
        (CHUNKS, enc_count, step_blocks, rows, NT), lambda i, *_: (0, 0, i, 0, 0)
    )
    attended, partial = pl.pallas_call(
        attend_kernel,
        out_shape=(
            jax.ShapeDtypeStruct(queries.shape, bf16),
            jax.ShapeDtypeStruct(whole.shape, bf16),
        ),
        grid_spec=pltpu.PrefetchScalarGridSpec(
            num_scalar_prefetch=2,
            grid=(spans // SPANS_PER_STEP,),
            in_specs=[
                by_blocks,
                by_rows,
                by_rows,
                pl.BlockSpec((enc_features, head_width), resident),
                pl.BlockSpec((enc_features, head_width), resident),
            ],
            out_specs=[by_rows, by_blocks],
            scratch_shapes=[
                pltpu.VMEM((head_width, step_blocks * NT), bf16),
            ]
            * 4
            + [pltpu.VMEM((head_width, enc_features), bf16)] * 2,
        ),
        compiler_params=params(dimension_semantics=("arbitrary",)),
    )(
        second_valid[0],
        live_spans,
        whole,
        queries,
        cotangent,
        key_weight,
        value_weight,
    )

    arrived = pl.pallas_call(
        functools.partial(return_kernel, enc_count, shard_count),
        out_shape=jax.ShapeDtypeStruct((CHUNKS, slot_total, rows, NT), bf16),
        in_specs=[SMEM, ANY],
        out_specs=ANY,
        scratch_shapes=[pltpu.VMEM((enc_count, used_count, rows, NT), bf16)] * CHUNKS
        + [pltpu.VMEM((used_count + 1, rows, NT), bf16)] * CHUNKS
        + [pltpu.VMEM((slot_total, rows, NT), bf16)] * CHUNKS
        + semaphores,
        compiler_params=params(collective_id=1, has_side_effects=True),
    )(place, partial)
    grad_store = pl.pallas_call(
        gather_kernel,
        out_shape=jax.ShapeDtypeStruct(store_rows.shape, jnp.float32),
        in_specs=[SMEM, VMEM, VMEM],
        out_specs=VMEM,
        scratch_shapes=[pltpu.VMEM((blocks_here, features, NT), jnp.float32)],
        compiler_params=params(),
    )(served, arrived, scale_wide)
    return (attended, grad_store.transpose(0, 2, 1))


def solution(mesh):
    return jax.shard_map(
        per_device,
        mesh=mesh,
        in_specs=(
            P("span", "enc"),
            P("span", "enc"),
            P(None, "enc"),
            P(None, "enc"),
            P("span", None, "enc"),
            P("span", None),
            P("span", None, None),
            P("span", None),
            P("span", None),
            P("span"),
        ),
        out_specs=(P("span", "enc"), P("span", None, "enc")),
        check_vma=False,
    )
```
